256 devices in a mesh: dp: 4 (over y), fsdp: 64 (over x, z, core).
Axes of the slice: x: 4, y: 4, z: 8, core: 2. Of those that a mesh axis runs over, the one named last changes fastest.
Arguments:
- grads: bfloat16 [4, 256, 512, 512], P('dp', None, 'fsdp'), may hold values from -6 to 6
- left_factor: float32 [256, 512, 512], P(('dp', 'fsdp')), as said below
- right_factor: float32 [256, 512, 512], P(('dp', 'fsdp')), as said below
- left_root: float32 [256, 512, 512], P(('dp', 'fsdp')), as said below
- right_root: float32 [256, 512, 512], P(('dp', 'fsdp')), as said below
- block_of_slot: int32 [256], replicated, may hold values from 0 to 255, as said below
- refresh: int32 [1], replicated, may hold values from 0 to 15
Outputs:
- new_left_factor: float32 [256, 512, 512], P(('dp', 'fsdp'))
- new_right_factor: float32 [256, 512, 512], P(('dp', 'fsdp'))
- new_left_root: float32 [256, 512, 512], P(('dp', 'fsdp'))
- new_right_root: float32 [256, 512, 512], P(('dp', 'fsdp'))
- update: bfloat16 [256, 512, 512], P(None, 'fsdp')
The draws below stay inside these ranges and needn't reach their ends.
Inputs may be any that keep to these rules, and one draw needn't show every extreme that they name: A permutation of the block numbers with block_of_slot[s] mod 16 equal to s mod 16 for every slot s. `left_factor`: every block is symmetric positive definite. `right_factor`: every block is symmetric positive definite. `left_root`: every block is symmetric. `right_root`: every block is symmetric.
All inputs are finite; a program needn't handle non-finite values.
Results may differ from the reference program's by a relative error of at most 0.015.
Values may be sent and summed in bfloat16 or wider, within the bound.
No kernel may reach another device: no remote copies, remote signals or barrier semaphores. Data moves between devices by JAX's collectives and lax.ppermute only.
A program may use at most 64 MiB of HBM per device.

```python
import math
import jax
import jax.numpy as jnp
from jax import lax

B = 512
ITERS = 2
NB = 256
N_DP = 4


def dominant_blocks(base_key, lowest, highest):
    diag_key, size_key, sign_key = jax.random.split(base_key, 3)
    diagonal = jnp.exp(jax.random.uniform(diag_key, (NB, B), jnp.float32, math.log(lowest), math.log(highest)))
    magnitude = jax.random.uniform(size_key, (NB, B, B), jnp.float32, 0.5, 1.0)
    sign_draw = jnp.where(jax.random.uniform(sign_key, (NB, B, B), jnp.float32) < 0.5, -1.0, 1.0)
    upper_part = jnp.triu(magnitude * sign_draw, 1)
    symmetric = upper_part + jnp.swapaxes(upper_part, 1, 2)
    spread = jnp.sqrt(diagonal)
    weight = 0.9 / math.sqrt(highest / lowest) / B
    off_diagonal = weight * symmetric * spread[:, :, None] * spread[:, None, :]
    return off_diagonal + diagonal[:, :, None] * jnp.eye(B, dtype=jnp.float32)


def draw_left_factor(key, part):
    key = jax.random.fold_in(key, 1)
    return dominant_blocks(key, 1.0, 10.0)


def draw_right_factor(key, part):
    key = jax.random.fold_in(key, 2)
    return dominant_blocks(key, 1.0, 10.0)


def draw_left_root(key, part):
    key = jax.random.fold_in(key, 3)
    return dominant_blocks(key, 0.3, 1.0)


def draw_right_root(key, part):
    key = jax.random.fold_in(key, 4)
    return dominant_blocks(key, 0.3, 1.0)


def draw_block_of_slot(key, part):
    key = jax.random.fold_in(key, 5)
    classes = NB // 16
    class_perms = [jax.random.permutation(jax.random.fold_in(key, residue), classes) for residue in range(16)]
    slot_table = 16 * jnp.stack(class_perms, axis=1) + jnp.arange(16)[None, :]
    return slot_table.reshape(NB).astype(jnp.int32)


def block_scale(own_key, dims, cuts, low, high):
    def one(position, shards_of):
        heights = jax.random.uniform(jax.random.fold_in(jax.random.fold_in(own_key, 6), position), (shards_of,), jnp.float32, low / len(cuts), high / len(cuts))
        return jnp.repeat(jnp.exp(heights), dims[position] // shards_of).reshape((-1,) + (1,) * (len(dims) - position - 1))

    level = one(*cuts[0])
    for cut in cuts[1:]:
        level = level * one(*cut)
    return level


def normal_values(stream_key, extent, width, reach, cuts=(), kind=jnp.bfloat16):
    array = jax.random.normal(stream_key, extent, jnp.float32) * width
    if len(cuts) > 0:
        array = block_scale(stream_key, extent, cuts, -0.22, 0.18) * array
    return jnp.clip(array, min=-reach, max=reach).astype(kind)


def setup_inputs(seed: int = 0) -> dict:
    key_of = jax.random.split(jax.random.key(seed), 8)
    return {
        "grads": normal_values(key_of[0], (N_DP, NB, B, B), 1.0, 6.0, ((0, 4), (2, 64))),
        "left_factor": draw_left_factor(jax.random.fold_in(key_of[7], 71), 0),
        "right_factor": draw_right_factor(jax.random.fold_in(key_of[7], 71), 0),
        "left_root": draw_left_root(jax.random.fold_in(key_of[7], 71), 0),
        "right_root": draw_right_root(jax.random.fold_in(key_of[7], 71), 0),
        "block_of_slot": draw_block_of_slot(jax.random.fold_in(key_of[7], 71), 0),
        "refresh": jax.random.randint(key_of[6], (1,), 0, 16).astype(jnp.int32),
    }


root_power = 4.0
refresh_period = 16
exact = lax.Precision.HIGHEST

def product(first_matrix, second_matrix):
    return jnp.dot(first_matrix, second_matrix, precision=exact, preferred_element_type=jnp.float32)

def inverse_root(factor):
    block_order = factor.shape[0]
    identity = jnp.eye(block_order, dtype=jnp.float32)
    scaling = (1.0 + root_power) / (2.0 * jnp.sqrt(jnp.sum(factor * factor)))
    approx = identity * scaling ** (1.0 / root_power)
    coupled = factor * scaling
    for iteration in range(ITERS):
        middle = ((root_power + 1.0) * identity - coupled) / root_power
        approx = product(approx, middle)
        square = product(middle, middle)
        coupled = product(product(square, square), coupled)
    return approx

def refreshed(factor, previous):
    return inverse_root(factor)

def kept(factor, previous):
    return previous

def reference(grads, left_factor, right_factor, left_root, right_root, block_of_slot, refresh):
    summed = lax.optimization_barrier(jnp.sum(grads, axis=0, dtype=jnp.float32))
    slot_grads = jnp.take(summed, block_of_slot, axis=0)
    chosen = block_of_slot % refresh_period == refresh[0]

    def one_slot(operands):
        grad_block, left_old, right_old, left_prev, right_prev, refresh_flag = operands
        left_new = left_old + product(grad_block, grad_block.T) / B
        right_new = right_old + product(grad_block.T, grad_block) / B
        left_now = lax.cond(refresh_flag, refreshed, kept, left_new, left_prev)
        right_now = lax.cond(refresh_flag, refreshed, kept, right_new, right_prev)
        preconditioned = product(product(left_now, grad_block), right_now).astype(jnp.bfloat16)
        return (left_new, right_new, left_now, right_now, preconditioned)
    results = lax.map(one_slot, (slot_grads, left_factor, right_factor, left_root, right_root, chosen))
    updates = jnp.zeros_like(results[4]).at[block_of_slot].set(results[4])
    return (results[0], results[1], results[2], results[3], updates)
```

```python
import functools

import jax
import jax.numpy as jnp
from jax import lax
from jax.experimental import pallas as pl
from jax.experimental.pallas import tpu as pltpu
from jax.sharding import PartitionSpec as P

ITERS = 2
REFRESH_PERIOD = 16
N_DP = 4

VMEM = pltpu.VMEM
SMEM = pltpu.SMEM


def bf16_dot(a, b, dims=((1,), (0,))):
    return lax.dot_general(
        a.astype(jnp.bfloat16),
        b.astype(jnp.bfloat16),
        (dims, ((), ())),
        preferred_element_type=jnp.float32,
    )


def take_kernel(index_ref, source_ref, out_ref):
    def body(slot, carry):
        out_ref[slot] = source_ref[index_ref[slot]]
        return carry

    lax.fori_loop(0, out_ref.shape[0], body, 0, unroll=8)


def take_blocks(index, source):
    return pl.pallas_call(
        take_kernel,
        out_shape=jax.ShapeDtypeStruct(source.shape, source.dtype),
        in_specs=[pl.BlockSpec(memory_space=SMEM), pl.BlockSpec(memory_space=VMEM)],
        out_specs=pl.BlockSpec(memory_space=VMEM),
        compiler_params=pltpu.CompilerParams(vmem_limit_bytes=16 * 2**20),
        name="order_blocks",
    )(index, source)


def spread_kernel(index_ref, start_ref, *refs):
    out_ref = refs[-1]
    for part, source_ref in enumerate(refs[:-1]):
        start = start_ref[part]

        def body(slot, carry):
            out_ref[index_ref[start + slot]] = source_ref[slot]
            return carry

        lax.fori_loop(0, source_ref.shape[0], body, 0, unroll=8)


def spread_blocks(index, starts, sources):
    rows, columns = sources[0].shape[1:]
    return pl.pallas_call(
        spread_kernel,
        out_shape=jax.ShapeDtypeStruct((index.shape[0], rows, columns), sources[0].dtype),
        in_specs=[pl.BlockSpec(memory_space=SMEM)] * 2
        + [pl.BlockSpec(memory_space=VMEM)] * len(sources),
        out_specs=pl.BlockSpec(memory_space=VMEM),
        compiler_params=pltpu.CompilerParams(vmem_limit_bytes=16 * 2**20),
        name="place_blocks",
    )(index, starts, *sources)


def inverse_root(factor):
    order = factor.shape[0]
    rows = lax.broadcasted_iota(jnp.int32, (order, order), 0)
    cols = lax.broadcasted_iota(jnp.int32, (order, order), 1)
    scaling = 2.5 / jnp.sqrt(jnp.sum(factor * factor, keepdims=True))
    root_scale = jnp.sqrt(jnp.sqrt(scaling))
    coupled = factor * scaling
    first = coupled * 0.25
    f_part = 2.5 * first - bf16_dot(first, first)
    h_part = 3.125 * f_part - bf16_dot(f_part, f_part)
    coupled = (1.5625 * 1.5625) * coupled - bf16_dot(h_part, coupled)
    second = coupled * 0.25
    total = bf16_dot(first, second) - 1.25 * (first + second)
    total = jnp.where(rows == cols, total + 1.5625, total)
    return total * root_scale


def owner_kernel(
    flag_ref, grad_ref, left_ref, right_ref, lroot_ref, rroot_ref,
    new_left_ref, new_right_ref, new_lroot_ref, new_rroot_ref, update_ref,
):
    order = grad_ref.shape[0]
    grad = grad_ref[...]
    new_left_ref[...] = left_ref[...] + bf16_dot(grad, grad, ((1,), (1,))) * (1.0 / order)
    new_right_ref[...] = right_ref[...] + bf16_dot(grad, grad, ((0,), (0,))) * (1.0 / order)

    @pl.when(flag_ref[0] != 0)
    def _():
        new_lroot_ref[...] = inverse_root(new_left_ref[...])
        new_rroot_ref[...] = inverse_root(new_right_ref[...])

    @pl.when(flag_ref[0] == 0)
    def _():
        new_lroot_ref[...] = lroot_ref[...]
        new_rroot_ref[...] = rroot_ref[...]

    mixed = bf16_dot(new_lroot_ref[...], grad)
    update_ref[...] = bf16_dot(mixed, new_rroot_ref[...]).astype(update_ref.dtype)


def owner_step(flag, grad, left, right, lroot, rroot):
    order = grad.shape[0]
    matrix = jax.ShapeDtypeStruct((order, order), jnp.float32)
    return pl.pallas_call(
        owner_kernel,
        out_shape=(matrix,) * 4 + (jax.ShapeDtypeStruct((order, order), jnp.bfloat16),),
        in_specs=[pl.BlockSpec(memory_space=SMEM)] + [pl.BlockSpec(memory_space=VMEM)] * 5,
        out_specs=(pl.BlockSpec(memory_space=VMEM),) * 5,
        compiler_params=pltpu.CompilerParams(vmem_limit_bytes=40 * 2**20),
        name="owner_step",
    )(flag, grad, left, right, lroot, rroot)


def per_device(grads, left_factor, right_factor, left_root, right_root, block_of_slot, refresh):
    shard_count = lax.axis_size("fsdp")
    data_count = lax.axis_size("dp")
    local = grads[0]
    blocks, piece_rows, order = local.shape
    me_dp, me_fsdp = lax.axis_index("dp"), lax.axis_index("fsdp")

    ordered = take_blocks(block_of_slot, local)
    ordered = ordered.reshape(data_count, blocks // data_count, piece_rows, order)
    replicas = lax.all_to_all(ordered, "dp", split_axis=0, concat_axis=0, tiled=True)
    summed = jnp.sum(replicas.astype(jnp.float32), axis=0).astype(jnp.bfloat16)
    grad = lax.all_to_all(summed, "fsdp", split_axis=0, concat_axis=0, tiled=True)
    grad = grad.reshape(order, order)

    own = lax.dynamic_slice_in_dim(block_of_slot, me_dp * shard_count + me_fsdp, 1)
    flag = (own % REFRESH_PERIOD == refresh).astype(jnp.int32)
    new_left, new_right, new_lroot, new_rroot, update = owner_step(
        flag, grad, left_factor[0], right_factor[0], left_root[0], right_root[0]
    )

    rows = update.reshape(shard_count, piece_rows, order)
    rows = lax.all_to_all(rows, "fsdp", split_axis=0, concat_axis=0, tiled=True)
    parts, starts = [rows], [me_dp * shard_count]
    for step in range(1, data_count):
        pairs = [(i, (i + step) % data_count) for i in range(data_count)]
        parts.append(lax.ppermute(rows, "dp", pairs))
        starts.append((me_dp + data_count - step) % data_count * shard_count)
    updates = spread_blocks(block_of_slot, jnp.stack(starts).astype(jnp.int32), parts)
    return new_left[None], new_right[None], new_lroot[None], new_rroot[None], updates


def solution(mesh):
    owned = P(("dp", "fsdp"), None, None)
    return jax.shard_map(
        per_device,
        mesh=mesh,
        in_specs=(P("dp", None, "fsdp", None), owned, owned, owned, owned, P(), P()),
        out_specs=(owned, owned, owned, owned, P(None, "fsdp", None)),
        check_vma=False,
    )
```

```python
import functools

import jax
import jax.numpy as jnp
from jax import lax
from jax.experimental import pallas as pl
from jax.experimental.pallas import tpu as pltpu
from jax.sharding import PartitionSpec as P

ITERS = 2
REFRESH_PERIOD = 16
N_DP = 4

VMEM = pltpu.VMEM
SMEM = pltpu.SMEM
HBM = pltpu.HBM


def bf16_dot(a, b, dims=((1,), (0,))):
    return lax.dot_general(
        a.astype(jnp.bfloat16),
        b.astype(jnp.bfloat16),
        (dims, ((), ())),
        preferred_element_type=jnp.float32,
    )


def order_kernel(pieces, index_ref, source_ref, *refs):
    outs, (index_smem, index_sem, sems) = refs[: len(pieces)], refs[len(pieces) :]
    fetch = pltpu.make_async_copy(index_ref, index_smem, index_sem)
    fetch.start()
    me = lax.axis_index("dp")
    fetch.wait()
    for number, ((quarter, first), out_ref) in enumerate(zip(pieces, outs, strict=True)):
        start = lax.rem(me + quarter, N_DP) * (index_ref.shape[0] // N_DP) + first

        def body(slot, carry, out_ref=out_ref, number=number, start=start):
            pltpu.make_async_copy(
                source_ref.at[index_smem[start + slot]], out_ref.at[slot], sems.at[number]
            ).start()
            return carry

        lax.fori_loop(0, out_ref.shape[0], body, 0, unroll=8)
    for number, out_ref in enumerate(outs):
        pltpu.make_async_copy(out_ref, out_ref, sems.at[number]).wait()


def order_blocks(index, source, pieces, counts, name):
    return pl.pallas_call(
        functools.partial(order_kernel, pieces),
        out_shape=[
            jax.ShapeDtypeStruct((count, *source.shape[1:]), source.dtype) for count in counts
        ],
        in_specs=[pl.BlockSpec(memory_space=HBM)] * 2,
        out_specs=[pl.BlockSpec(memory_space=pl.ANY)] * len(pieces),
        scratch_shapes=[
            pltpu.SMEM(index.shape, index.dtype),
            pltpu.SemaphoreType.DMA,
            pltpu.SemaphoreType.DMA((len(pieces),)),
        ],
        compiler_params=pltpu.CompilerParams(vmem_limit_bytes=4 * 2**20),
        name=name,
    )(index, source)


def place_kernel(pieces, index_ref, *refs):
    out_ref = refs[-1]
    me = lax.axis_index("dp")
    for (quarter, first), source_ref in zip(pieces, refs[:-1], strict=True):
        start = lax.rem(me + quarter, N_DP) * (index_ref.shape[0] // N_DP) + first

        def body(slot, carry, source_ref=source_ref, start=start):
            out_ref[index_ref[start + slot]] = source_ref[slot]
            return carry

        lax.fori_loop(0, source_ref.shape[0], body, 0, unroll=8)


def place_blocks(index, sources, pieces):
    rows, columns = sources[0].shape[1:]
    return pl.pallas_call(
        functools.partial(place_kernel, pieces),
        out_shape=jax.ShapeDtypeStruct((index.shape[0], rows, columns), sources[0].dtype),
        in_specs=[pl.BlockSpec(memory_space=SMEM)]
        + [pl.BlockSpec(memory_space=VMEM)] * len(sources),
        out_specs=pl.BlockSpec(memory_space=VMEM),
        compiler_params=pltpu.CompilerParams(vmem_limit_bytes=8 * 2**20),
        name="place_blocks",
    )(index, *sources)


def add_kernel(first_ref, second_ref, out_ref):
    total = first_ref[...].astype(jnp.float32) + second_ref[...].astype(jnp.float32)
    out_ref[...] = total.astype(out_ref.dtype)


def add_pieces(first, second):
    return pl.pallas_call(
        add_kernel,
        out_shape=jax.ShapeDtypeStruct(first.shape, first.dtype),
        in_specs=[pl.BlockSpec(memory_space=VMEM)] * 2,
        out_specs=pl.BlockSpec(memory_space=VMEM),
        compiler_params=pltpu.CompilerParams(vmem_limit_bytes=4 * 2**20),
        name="add_pieces",
    )(first, second)


def total_kernel(mine_ref, comb_a_ref, raw_a_ref, comb_b_ref, raw_b_ref, out_ref):
    half = comb_a_ref.shape[0]
    for start, comb_ref, raw_ref in ((0, comb_a_ref, raw_a_ref), (half, comb_b_ref, raw_b_ref)):
        part = pl.ds(start, half)
        total = mine_ref[part].astype(jnp.float32) + comb_ref[...].astype(jnp.float32)
        out_ref[part] = (total + raw_ref[...].astype(jnp.float32)).astype(out_ref.dtype)


def total_pieces(*pieces):
    return pl.pallas_call(
        total_kernel,
        out_shape=jax.ShapeDtypeStruct(pieces[0].shape, pieces[0].dtype),
        in_specs=[pl.BlockSpec(memory_space=VMEM)] * 5,
        out_specs=pl.BlockSpec(memory_space=VMEM),
        compiler_params=pltpu.CompilerParams(vmem_limit_bytes=6 * 2**20),
        name="total_pieces",
    )(*pieces)


def inverse_root(factor):
    order = factor.shape[0]
    rows = lax.broadcasted_iota(jnp.int32, (order, order), 0)
    cols = lax.broadcasted_iota(jnp.int32, (order, order), 1)
    scaling = 2.5 / jnp.sqrt(jnp.sum(factor * factor, keepdims=True))
    root_scale = jnp.sqrt(jnp.sqrt(scaling))
    coupled = factor * scaling
    first = coupled * 0.25
    f_part = 2.5 * first - bf16_dot(first, first)
    h_part = 3.125 * f_part - bf16_dot(f_part, f_part)
    coupled = (1.5625 * 1.5625) * coupled - bf16_dot(h_part, coupled)
    second = coupled * 0.25
    total = bf16_dot(first, second) - 1.25 * (first + second)
    total = jnp.where(rows == cols, total + 1.5625, total)
    return total * root_scale


def owner_kernel(
    flag_ref, grad_ref, left_ref, right_ref, lroot_ref, rroot_ref,
    new_left_ref, new_right_ref, new_lroot_ref, new_rroot_ref, update_ref,
):
    order = grad_ref.shape[0]
    grad = grad_ref[...]
    new_left_ref[...] = left_ref[...] + bf16_dot(grad, grad, ((1,), (1,))) * (1.0 / order)
    new_right_ref[...] = right_ref[...] + bf16_dot(grad, grad, ((0,), (0,))) * (1.0 / order)

    @pl.when(flag_ref[0] != 0)
    def _():
        new_lroot_ref[...] = inverse_root(new_left_ref[...])
        new_rroot_ref[...] = inverse_root(new_right_ref[...])

    @pl.when(flag_ref[0] == 0)
    def _():
        new_lroot_ref[...] = lroot_ref[...]
        new_rroot_ref[...] = rroot_ref[...]

    mixed = bf16_dot(new_lroot_ref[...], grad)
    update_ref[...] = bf16_dot(mixed, new_rroot_ref[...]).astype(update_ref.dtype)


def owner_step(flag, grad, left, right, lroot, rroot):
    order = grad.shape[0]
    matrix = jax.ShapeDtypeStruct((order, order), jnp.float32)
    return pl.pallas_call(
        owner_kernel,
        out_shape=(matrix,) * 4 + (jax.ShapeDtypeStruct((order, order), jnp.bfloat16),),
        in_specs=[pl.BlockSpec(memory_space=SMEM)] + [pl.BlockSpec(memory_space=VMEM)] * 5,
        out_specs=(pl.BlockSpec(memory_space=VMEM),) * 5,
        compiler_params=pltpu.CompilerParams(vmem_limit_bytes=24 * 2**20),
        name="owner_step",
    )(flag, grad, left, right, lroot, rroot)


def per_device(grads, left_factor, right_factor, left_root, right_root, block_of_slot, refresh):
    shard_count = lax.axis_size("fsdp")
    local = grads[0]
    blocks, piece_rows, order = local.shape
    quarter, half = blocks // N_DP, blocks // N_DP // 2

    def to_next(piece):
        return lax.ppermute(piece, "dp", [(i, (i + 1) % N_DP) for i in range(N_DP)])

    def to_prev(piece):
        return lax.ppermute(piece, "dp", [(i, (i - 1) % N_DP) for i in range(N_DP)])

    relay_a, relay_b = order_blocks(
        block_of_slot, local, ((2, 0), (2, half)), (half, half), "order_relays"
    )
    own_a, own_b, raw_b, raw_a, mine = order_blocks(
        block_of_slot,
        local,
        ((1, 0), (3, half), (1, half), (3, 0), (0, 0)),
        (half, half, half, half, quarter),
        "order_rest",
    )
    relayed_a, relayed_b = to_next(relay_a), to_prev(relay_b)
    raw_a, raw_b = to_prev(raw_a), to_next(raw_b)
    comb_a, comb_b = to_next(add_pieces(own_a, relayed_a)), to_prev(add_pieces(own_b, relayed_b))
    summed = total_pieces(mine, comb_a, raw_a, comb_b, raw_b)

    grad = lax.all_to_all(summed, "fsdp", split_axis=0, concat_axis=0, tiled=True)
    grad = grad.reshape(order, order)

    own = lax.dynamic_slice_in_dim(
        block_of_slot, lax.axis_index("dp") * shard_count + lax.axis_index("fsdp"), 1
    )
    flag = (own % REFRESH_PERIOD == refresh).astype(jnp.int32)
    new_left, new_right, new_lroot, new_rroot, update = owner_step(
        flag, grad, left_factor[0], right_factor[0], left_root[0], right_root[0]
    )

    rows = update.reshape(shard_count, piece_rows, order)
    rows = lax.all_to_all(rows, "fsdp", split_axis=0, concat_axis=0, tiled=True)
    rows_a, rows_b = rows[:half], rows[half:]
    prev_a, next_b = to_next(rows_a), to_prev(rows_b)
    prev_b, next_a = to_next(rows_b), to_prev(rows_a)
    over_a, over_b = to_next(prev_a), to_prev(next_b)
    updates = place_blocks(
        block_of_slot,
        (rows, prev_a, prev_b, next_a, next_b, over_a, over_b),
        ((0, 0), (3, 0), (3, half), (1, 0), (1, half), (2, 0), (2, half)),
    )
    return new_left[None], new_right[None], new_lroot[None], new_rroot[None], updates


def solution(mesh):
    owned = P(("dp", "fsdp"), None, None)
    return jax.shard_map(
        per_device,
        mesh=mesh,
        in_specs=(P("dp", None, "fsdp", None), owned, owned, owned, owned, P(), P()),
        out_specs=(owned, owned, owned, owned, P(None, "fsdp", None)),
        check_vma=False,
    )
```

```python
import functools

import jax
import jax.numpy as jnp
from jax import lax
from jax.experimental import pallas as pl
from jax.experimental.pallas import tpu as pltpu
from jax.sharding import PartitionSpec as P

ITERS = 2
REFRESH_PERIOD = 16
N_DP = 4

VMEM = pltpu.VMEM
SMEM = pltpu.SMEM
HBM = pltpu.HBM


def bf16_dot(a, b, dims=((1,), (0,))):
    return lax.dot_general(
        a.astype(jnp.bfloat16),
        b.astype(jnp.bfloat16),
        (dims, ((), ())),
        preferred_element_type=jnp.float32,
    )


def piece_start(quarter, first, slots):
    return lax.rem(lax.axis_index("dp") + quarter, N_DP) * (slots // N_DP) + first


def copy_rows(index_smem, source_ref, out_ref, start):
    def body(slot, carry):
        out_ref[slot] = source_ref[index_smem[start + slot]]
        return carry

    lax.fori_loop(0, out_ref.shape[0], body, 0, unroll=8)


CHUNKS = 8


def order_first_kernel(pieces, index_ref, source_ref, held_ref, index_smem, *refs):
    outs, (index_sem, sems) = refs[: len(pieces)], refs[len(pieces) :]
    fetch = pltpu.make_async_copy(index_ref, index_smem, index_sem)
    fetch.start()
    count = source_ref.shape[0] // CHUNKS
    loads = [
        pltpu.make_async_copy(
            source_ref.at[pl.ds(i * count, count)], held_ref.at[pl.ds(i * count, count)], sems.at[i]
        )
        for i in range(CHUNKS)
    ]
    for load in loads:
        load.start()
    fetch.wait()
    for load in loads:
        load.wait()
    for (quarter, first), out_ref in zip(pieces, outs, strict=True):
        copy_rows(index_smem, held_ref, out_ref, piece_start(quarter, first, index_ref.shape[0]))


def order_rest_kernel(pieces, index_ref, refresh_ref, held_ref, refresh_smem, *outs):
    refresh_smem[0] = refresh_ref[0]
    for (quarter, first), out_ref in zip(pieces, outs, strict=True):
        copy_rows(index_ref, held_ref, out_ref, piece_start(quarter, first, index_ref.shape[0]))


def order_first(index, source, pieces, counts):
    tail = source.shape[1:]
    return pl.pallas_call(
        functools.partial(order_first_kernel, pieces),
        out_shape=[VMEM(source.shape, source.dtype), SMEM(index.shape, index.dtype)]
        + [VMEM((count, *tail), source.dtype) for count in counts],
        in_specs=[pl.BlockSpec(memory_space=HBM)] * 2,
        out_specs=[pl.BlockSpec(memory_space=VMEM), pl.BlockSpec(memory_space=SMEM)]
        + [pl.BlockSpec(memory_space=VMEM)] * len(pieces),
        scratch_shapes=[pltpu.SemaphoreType.DMA, pltpu.SemaphoreType.DMA((CHUNKS,))],
        compiler_params=pltpu.CompilerParams(vmem_limit_bytes=8 * 2**20),
        name="order_first",
    )(
        pltpu.with_memory_space_constraint(index, HBM),
        pltpu.with_memory_space_constraint(source, HBM),
    )


def order_rest(index, refresh, held, pieces, counts):
    return pl.pallas_call(
        functools.partial(order_rest_kernel, pieces),
        out_shape=[SMEM(refresh.shape, refresh.dtype)]
        + [VMEM((count, *held.shape[1:]), held.dtype) for count in counts],
        in_specs=[pl.BlockSpec(memory_space=space) for space in (SMEM, SMEM, VMEM)],
        out_specs=[pl.BlockSpec(memory_space=SMEM)]
        + [pl.BlockSpec(memory_space=VMEM)] * len(pieces),
        compiler_params=pltpu.CompilerParams(vmem_limit_bytes=8 * 2**20),
        name="order_rest",
    )(index, refresh, held)


def place_kernel(pieces, aliased, index_ref, *refs):
    sources = refs[: len(pieces)]
    out_ref, sems = refs[len(pieces) + aliased :]
    for number, ((quarter, first), source_ref) in enumerate(zip(pieces, sources, strict=True)):
        start = piece_start(quarter, first, index_ref.shape[0])

        def body(slot, carry, source_ref=source_ref, number=number, start=start):
            pltpu.make_async_copy(
                source_ref.at[slot], out_ref.at[index_ref[start + slot]], sems.at[number]
            ).start()
            return carry

        lax.fori_loop(0, source_ref.shape[0], body, 0, unroll=16)
    for number, source_ref in enumerate(sources):
        pltpu.make_async_copy(source_ref, source_ref, sems.at[number]).wait()


def place_blocks(index, sources, pieces, name, out=None):
    rows, columns = sources[0].shape[1:]
    aliased = 0 if out is None else 1
    return pl.pallas_call(
        functools.partial(place_kernel, pieces, aliased),
        out_shape=jax.ShapeDtypeStruct((index.shape[0], rows, columns), sources[0].dtype),
        in_specs=[pl.BlockSpec(memory_space=SMEM)]
        + [pl.BlockSpec(memory_space=pl.ANY)] * (len(sources) + aliased),
        out_specs=pl.BlockSpec(memory_space=pl.ANY),
        scratch_shapes=[pltpu.SemaphoreType.DMA((len(pieces),))],
        input_output_aliases={1 + len(sources): 0} if aliased else {},
        compiler_params=pltpu.CompilerParams(vmem_limit_bytes=4 * 2**20),
        cost_estimate=pl.CostEstimate(
            flops=0, bytes_accessed=64 * rows * columns * 64 * len(sources), transcendentals=0
        ),
        name=name,
    )(index, *sources, *(() if out is None else (out,)))


def add_kernel(first_ref, second_ref, out_ref):
    total = first_ref[...].astype(jnp.float32) + second_ref[...].astype(jnp.float32)
    out_ref[...] = total.astype(out_ref.dtype)


def add_pieces(first, second):
    return pl.pallas_call(
        add_kernel,
        out_shape=jax.ShapeDtypeStruct(first.shape, first.dtype),
        in_specs=[pl.BlockSpec(memory_space=VMEM)] * 2,
        out_specs=pl.BlockSpec(memory_space=VMEM),
        compiler_params=pltpu.CompilerParams(vmem_limit_bytes=4 * 2**20),
        name="add_pieces",
    )(first, second)


def partial_kernel(mine_ref, raw_a_ref, raw_b_ref, out_ref):
    half = raw_a_ref.shape[0]
    for start, raw_ref in ((0, raw_a_ref), (half, raw_b_ref)):
        part = pl.ds(start, half)
        out_ref[part] = mine_ref[part].astype(jnp.float32) + raw_ref[...].astype(jnp.float32)


def partial_sum(mine, raw_a, raw_b):
    return pl.pallas_call(
        partial_kernel,
        out_shape=VMEM(mine.shape, jnp.float32),
        in_specs=[pl.BlockSpec(memory_space=VMEM)] * 3,
        out_specs=pl.BlockSpec(memory_space=VMEM),
        compiler_params=pltpu.CompilerParams(vmem_limit_bytes=6 * 2**20),
        name="partial_sum",
    )(mine, raw_a, raw_b)


def total_kernel(tie_ref, partial_ref, comb_a_ref, comb_b_ref, out_ref):
    del tie_ref
    half = comb_a_ref.shape[0]
    for start, comb_ref in ((0, comb_a_ref), (half, comb_b_ref)):
        part = pl.ds(start, half)
        total = partial_ref[part] + comb_ref[...].astype(jnp.float32)
        out_ref[part] = total.astype(out_ref.dtype)


def total_sum(tie, partial, comb_a, comb_b):
    return pl.pallas_call(
        total_kernel,
        out_shape=VMEM(partial.shape, comb_a.dtype),
        in_specs=[pl.BlockSpec(memory_space=pl.ANY)] + [pl.BlockSpec(memory_space=VMEM)] * 3,
        out_specs=pl.BlockSpec(memory_space=VMEM),
        compiler_params=pltpu.CompilerParams(vmem_limit_bytes=6 * 2**20),
        name="total_sum",
    )(tie, partial, comb_a, comb_b)


def inverse_roots(factors):
    fifth = [1.25 ** (5 - k) * (-0.25) ** k * c for k, c in enumerate((1, 5, 10, 10, 5, 1))]
    coefficients = [1.5625, -0.3125, 0.0, 0.0, 0.0, 0.0, 0.0]
    for k, value in enumerate(fifth):
        coefficients[k + 1] -= value / 4
    order = factors[0].shape[0]
    rows = lax.broadcasted_iota(jnp.int32, (order, order), 0)
    cols = lax.broadcasted_iota(jnp.int32, (order, order), 1)
    norms = [jnp.sqrt(jnp.sum(factor * factor, keepdims=True)) for factor in factors]
    scalings = [2.5 / norm for norm in norms]
    once = [factor * scaling for factor, scaling in zip(factors, scalings)]
    twice = [bf16_dot(m, m) for m in once]
    thrice = [bf16_dot(m2, m) for m2, m in zip(twice, once)]
    p = coefficients
    roots = []
    for m, m2, m3, scaling in zip(once, twice, thrice, scalings):
        low = p[1] * m + p[2] * m2 + p[3] * m3
        high = p[4] * m + p[5] * m2 + p[6] * m3
        total = bf16_dot(high, m3) + low
        total = jnp.where(rows == cols, total + p[0], total)
        roots.append(total * jnp.sqrt(jnp.sqrt(scaling)))
    return roots


def refreshing(refresh_ref):
    mine = lax.axis_index("dp") * lax.axis_size("fsdp") + lax.axis_index("fsdp")
    return lax.rem(mine, REFRESH_PERIOD) == refresh_ref[0]


def load_kernel(tie_ref, *refs):
    del tie_ref
    count = len(refs) // 2
    loads = [
        pltpu.make_async_copy(refs[i], refs[count + i], refs[-1].at[i]) for i in range(count)
    ]
    for load in loads:
        load.start()
    for load in loads:
        load.wait()


def load_matrices(tie, *matrices):
    return pl.pallas_call(
        load_kernel,
        out_shape=[VMEM(m.shape, m.dtype) for m in matrices],
        in_specs=[pl.BlockSpec(memory_space=pl.ANY)] + [pl.BlockSpec(memory_space=HBM)] * len(matrices),
        out_specs=[pl.BlockSpec(memory_space=VMEM)] * len(matrices),
        scratch_shapes=[pltpu.SemaphoreType.DMA((len(matrices),))],
        compiler_params=pltpu.CompilerParams(vmem_limit_bytes=8 * 2**20),
        name="load_matrices",
    )(tie, *[pltpu.with_memory_space_constraint(m, HBM) for m in matrices])


def gram_rows(grad):
    return bf16_dot(grad, grad, ((1,), (1,))) * (1.0 / grad.shape[0])


def gram_columns(grad):
    return bf16_dot(grad, grad, ((0,), (0,))) * (1.0 / grad.shape[0])


def update_kernel(
    refresh_ref, grad_ref, left_ref, right_ref, lroot_ref, rroot_ref,
    new_lroot_ref, new_rroot_ref, update_ref, roots, sems,
):
    grad = grad_ref[...]
    refreshed = refreshing(refresh_ref)

    @pl.when(refreshed)
    def _():
        new_left = left_ref[...] + gram_rows(grad)
        new_right = right_ref[...] + gram_columns(grad)
        new_roots = inverse_roots((new_left, new_right))
        writes = []
        for i, (root, out_ref) in enumerate(zip(new_roots, (new_lroot_ref, new_rroot_ref))):
            roots[i] = root
            write = pltpu.make_async_copy(roots.at[i], out_ref, sems.at[i])
            write.start()
            writes.append(write)
        mixed = bf16_dot(roots[0], grad)
        update_ref[...] = bf16_dot(mixed, roots[1]).astype(update_ref.dtype)
        for write in writes:
            write.wait()

    @pl.when(jnp.logical_not(refreshed))
    def _():
        loads = [
            pltpu.make_async_copy(source, roots.at[i], sems.at[i])
            for i, source in enumerate((lroot_ref, rroot_ref))
        ]
        for load in loads:
            load.start()
        loads[0].wait()
        mixed = bf16_dot(roots[0], grad)
        loads[1].wait()
        update_ref[...] = bf16_dot(mixed, roots[1]).astype(update_ref.dtype)


def owner_update(refresh, grad, left, right, lroot, rroot):
    order = grad.shape[0]
    return pl.pallas_call(
        update_kernel,
        out_shape=(
            HBM((order, order), jnp.float32),
            HBM((order, order), jnp.float32),
            VMEM((order, order), jnp.bfloat16),
        ),
        in_specs=[pl.BlockSpec(memory_space=SMEM)]
        + [pl.BlockSpec(memory_space=VMEM)] * 3
        + [pl.BlockSpec(memory_space=HBM)] * 2,
        out_specs=(pl.BlockSpec(memory_space=HBM),) * 2 + (pl.BlockSpec(memory_space=VMEM),),
        scratch_shapes=[
            pltpu.VMEM((2, order, order), jnp.float32),
            pltpu.SemaphoreType.DMA((2,)),
        ],
        compiler_params=pltpu.CompilerParams(vmem_limit_bytes=24 * 2**20),
        name="owner_update",
    )(refresh, grad, left, right, lroot, rroot)


def factors_kernel(
    tie_ref, refresh_ref, grad_ref, left_ref, right_ref, lroot_ref, rroot_ref, old_l_ref, old_r_ref,
    new_left_ref, new_right_ref, new_lroot_ref, new_rroot_ref,
    left, right, roots, sems,
):
    del tie_ref, old_l_ref, old_r_ref
    kept = jnp.logical_not(refreshing(refresh_ref))
    loads = [
        pltpu.make_async_copy(source, roots.at[i], sems.at[2 + i])
        for i, source in enumerate((lroot_ref, rroot_ref))
    ]
    keeps = [
        pltpu.make_async_copy(roots.at[i], target, sems.at[2 + i])
        for i, target in enumerate((new_lroot_ref, new_rroot_ref))
    ]

    @pl.when(kept)
    def _():
        for load in loads:
            load.start()

    grad = grad_ref[...]
    left[...] = left_ref[...] + gram_rows(grad)
    write_left = pltpu.make_async_copy(left, new_left_ref, sems.at[0])
    write_left.start()
    right[...] = right_ref[...] + gram_columns(grad)
    write_right = pltpu.make_async_copy(right, new_right_ref, sems.at[1])
    write_right.start()

    @pl.when(kept)
    def _():
        for load, keep in zip(loads, keeps, strict=True):
            load.wait()
            keep.start()
        for keep in keeps:
            keep.wait()

    write_left.wait()
    write_right.wait()


def owner_factors(tie, refresh, grad, left, right, lroot, rroot, new_lroot, new_rroot):
    order = grad.shape[0]
    return pl.pallas_call(
        factors_kernel,
        out_shape=(HBM((order, order), jnp.float32),) * 4,
        in_specs=[pl.BlockSpec(memory_space=pl.ANY), pl.BlockSpec(memory_space=SMEM)]
        + [pl.BlockSpec(memory_space=VMEM)] * 3
        + [pl.BlockSpec(memory_space=HBM)] * 4,
        out_specs=(pl.BlockSpec(memory_space=HBM),) * 4,
        scratch_shapes=[pltpu.VMEM((order, order), jnp.float32)] * 2
        + [pltpu.VMEM((2, order, order), jnp.float32), pltpu.SemaphoreType.DMA((4,))],
        input_output_aliases={7: 2, 8: 3},
        compiler_params=pltpu.CompilerParams(vmem_limit_bytes=16 * 2**20),
        name="owner_factors",
    )(
        tie,
        refresh,
        grad, left, right, lroot, rroot, new_lroot, new_rroot,
    )


def per_device(grads, left_factor, right_factor, left_root, right_root, block_of_slot, refresh):
    shard_count = lax.axis_size("fsdp")
    local = grads[0]
    blocks, piece_rows, order = local.shape
    quarter, half = blocks // N_DP, blocks // N_DP // 2

    def to_next(piece):
        return lax.ppermute(piece, "dp", [(i, (i + 1) % N_DP) for i in range(N_DP)])

    def to_prev(piece):
        return lax.ppermute(piece, "dp", [(i, (i - 1) % N_DP) for i in range(N_DP)])

    held, index, relay_a, relay_b = order_first(
        block_of_slot, local, ((2, 0), (2, half)), (half, half)
    )
    relayed_a, relayed_b = to_next(relay_a), to_prev(relay_b)
    refresh, raw_a, raw_b, own_a, own_b, mine = order_rest(
        index,
        refresh,
        held,
        ((3, 0), (1, half), (1, 0), (3, half), (0, 0)),
        (half, half, half, half, quarter),
    )
    raw_a, raw_b = to_prev(raw_a), to_next(raw_b)
    sum_a, sum_b = add_pieces(own_a, relayed_a), add_pieces(own_b, relayed_b)
    comb_a, comb_b = to_next(sum_a), to_prev(sum_b)
    left, right = load_matrices(sum_b, left_factor[0], right_factor[0])
    lroot, rroot = (
        pltpu.with_memory_space_constraint(root[0], HBM) for root in (left_root, right_root)
    )
    summed = total_sum(left, partial_sum(mine, raw_a, raw_b), comb_a, comb_b)

    grad = lax.all_to_all(summed, "fsdp", split_axis=0, concat_axis=0, tiled=True)
    grad = grad.reshape(order, order)

    new_lroot, new_rroot, update = owner_update(refresh, grad, left, right, lroot, rroot)

    rows = update.reshape(shard_count, piece_rows, order)
    rows = lax.all_to_all(rows, "fsdp", split_axis=0, concat_axis=0, tiled=True)
    rows_a, rows_b = rows[:half], rows[half:]
    prev_a, next_b = to_next(rows_a), to_prev(rows_b)
    prev_b, next_a = to_next(rows_b), to_prev(rows_a)
    new_left, new_right, new_lroot, new_rroot = owner_factors(
        rows_a, refresh, grad, left, right, lroot, rroot, new_lroot, new_rroot
    )
    over_a, over_b = to_next(prev_a), to_prev(next_b)
    updates = place_blocks(
        index,
        (rows, prev_a, next_b, prev_b, next_a),
        ((0, 0), (3, 0), (1, half), (3, half), (1, 0)),
        "place_early",
    )
    updates = place_blocks(
        index, (over_a, over_b), ((2, 0), (2, half)), "place_late", updates
    )
    return new_left[None], new_right[None], new_lroot[None], new_rroot[None], updates


def solution(mesh):
    owned = P(("dp", "fsdp"), None, None)
    return jax.shard_map(
        per_device,
        mesh=mesh,
        in_specs=(P("dp", None, "fsdp", None), owned, owned, owned, owned, P(), P()),
        out_specs=(owned, owned, owned, owned, P(None, "fsdp", None)),
        check_vma=False,
    )
```

```python
import functools

import jax
import jax.numpy as jnp
from jax import lax
from jax.experimental import pallas as pl
from jax.experimental.pallas import tpu as pltpu
from jax.sharding import PartitionSpec as P

ITERS = 2
REFRESH_PERIOD = 16
N_DP = 4

VMEM = pltpu.VMEM
SMEM = pltpu.SMEM
HBM = pltpu.HBM


def bf16_dot(a, b, dims=((1,), (0,))):
    return lax.dot_general(
        a.astype(jnp.bfloat16),
        b.astype(jnp.bfloat16),
        (dims, ((), ())),
        preferred_element_type=jnp.float32,
    )


def core_index():
    return lax.rem(lax.axis_index("fsdp"), 2)


def piece_slots(quarter, parity, slots):
    start = lax.rem(lax.axis_index("dp") + quarter, N_DP) * (slots // N_DP)
    return start + lax.rem(core_index() + parity, 2)


def copy_rows(index_smem, source_ref, out_ref, start):
    def body(slot, carry):
        out_ref[slot] = source_ref[index_smem[start + 2 * slot]]
        return carry

    lax.fori_loop(0, out_ref.shape[0], body, 0, unroll=8)


CHUNKS = 8


def order_first_kernel(pieces, index_ref, source_ref, held_ref, index_smem, *refs):
    outs, (index_sem, sems) = refs[: len(pieces)], refs[len(pieces) :]
    fetch = pltpu.make_async_copy(index_ref, index_smem, index_sem)
    fetch.start()
    count = source_ref.shape[0] // CHUNKS
    loads = [
        pltpu.make_async_copy(
            source_ref.at[pl.ds(i * count, count)], held_ref.at[pl.ds(i * count, count)], sems.at[i]
        )
        for i in range(CHUNKS)
    ]
    for load in loads:
        load.start()
    fetch.wait()
    for load in loads:
        load.wait()
    for (quarter, parity), out_ref in zip(pieces, outs, strict=True):
        copy_rows(index_smem, held_ref, out_ref, piece_slots(quarter, parity, index_ref.shape[0]))


def order_rest_kernel(pieces, index_ref, refresh_ref, held_ref, refresh_smem, *outs):
    refresh_smem[0] = refresh_ref[0]
    for (quarter, parity), out_ref in zip(pieces, outs, strict=True):
        copy_rows(index_ref, held_ref, out_ref, piece_slots(quarter, parity, index_ref.shape[0]))


def order_first(index, source, pieces):
    piece = (source.shape[0] // N_DP // 2, *source.shape[1:])
    return pl.pallas_call(
        functools.partial(order_first_kernel, pieces),
        out_shape=[VMEM(source.shape, source.dtype), SMEM(index.shape, index.dtype)]
        + [VMEM(piece, source.dtype) for _ in pieces],
        in_specs=[pl.BlockSpec(memory_space=HBM)] * 2,
        out_specs=[pl.BlockSpec(memory_space=VMEM), pl.BlockSpec(memory_space=SMEM)]
        + [pl.BlockSpec(memory_space=VMEM)] * len(pieces),
        scratch_shapes=[pltpu.SemaphoreType.DMA, pltpu.SemaphoreType.DMA((CHUNKS,))],
        compiler_params=pltpu.CompilerParams(vmem_limit_bytes=8 * 2**20),
        name="order_first",
    )(
        pltpu.with_memory_space_constraint(index, HBM),
        pltpu.with_memory_space_constraint(source, HBM),
    )


def order_rest(index, refresh, held, pieces):
    piece = (held.shape[0] // N_DP // 2, *held.shape[1:])
    return pl.pallas_call(
        functools.partial(order_rest_kernel, pieces),
        out_shape=[SMEM(refresh.shape, refresh.dtype)]
        + [VMEM(piece, held.dtype) for _ in pieces],
        in_specs=[pl.BlockSpec(memory_space=space) for space in (SMEM, SMEM, VMEM)],
        out_specs=[pl.BlockSpec(memory_space=SMEM)]
        + [pl.BlockSpec(memory_space=VMEM)] * len(pieces),
        compiler_params=pltpu.CompilerParams(vmem_limit_bytes=8 * 2**20),
        name="order_rest",
    )(index, refresh, held)


def place_kernel(pieces, aliased, index_ref, *refs):
    sources = refs[: len(pieces)]
    out_ref, sems = refs[len(pieces) + aliased :]
    for number, ((quarter, parity), source_ref) in enumerate(zip(pieces, sources, strict=True)):
        start = piece_slots(quarter, parity, index_ref.shape[0])

        def body(slot, carry, source_ref=source_ref, number=number, start=start):
            pltpu.make_async_copy(
                source_ref.at[slot], out_ref.at[index_ref[start + 2 * slot]], sems.at[number]
            ).start()
            return carry

        lax.fori_loop(0, source_ref.shape[0], body, 0, unroll=16)
    for number, source_ref in enumerate(sources):
        pltpu.make_async_copy(source_ref, source_ref, sems.at[number]).wait()


def place_blocks(index, sources, pieces, name, out=None):
    rows, columns = sources[0].shape[1:]
    aliased = 0 if out is None else 1
    return pl.pallas_call(
        functools.partial(place_kernel, pieces, aliased),
        out_shape=jax.ShapeDtypeStruct((index.shape[0], rows, columns), sources[0].dtype),
        in_specs=[pl.BlockSpec(memory_space=SMEM)]
        + [pl.BlockSpec(memory_space=pl.ANY)] * (len(sources) + aliased),
        out_specs=pl.BlockSpec(memory_space=pl.ANY),
        scratch_shapes=[pltpu.SemaphoreType.DMA((len(pieces),))],
        input_output_aliases={1 + len(sources): 0} if aliased else {},
        compiler_params=pltpu.CompilerParams(vmem_limit_bytes=4 * 2**20),
        cost_estimate=pl.CostEstimate(
            flops=0, bytes_accessed=64 * rows * columns * 64 * len(sources), transcendentals=0
        ),
        name=name,
    )(index, *sources, *(() if out is None else (out,)))


def add_kernel(*refs):
    total = refs[0][...].astype(jnp.float32) + refs[1][...].astype(jnp.float32)
    refs[-1][...] = total.astype(refs[-1].dtype)


def add_pieces(first, second, dtype, name, tie=None):
    ties = () if tie is None else (tie,)
    return pl.pallas_call(
        add_kernel,
        out_shape=VMEM(first.shape, dtype),
        in_specs=[pl.BlockSpec(memory_space=VMEM)] * 2
        + [pl.BlockSpec(memory_space=pl.ANY)] * len(ties),
        out_specs=pl.BlockSpec(memory_space=VMEM),
        compiler_params=pltpu.CompilerParams(vmem_limit_bytes=6 * 2**20),
        name=name,
    )(first, second, *ties)


def join_kernel(partial_ref, comb_ref, other_ref, out_ref):
    me = core_index()
    total = partial_ref[...] + comb_ref[...].astype(jnp.float32)
    out_ref[:, me] = total.astype(out_ref.dtype)
    out_ref[:, 1 - me] = other_ref[...]


def join_cores(partial, comb, other):
    slots, rows, columns = comb.shape
    return pl.pallas_call(
        join_kernel,
        out_shape=VMEM((slots, 2, rows, columns), comb.dtype),
        in_specs=[pl.BlockSpec(memory_space=VMEM)] * 3,
        out_specs=pl.BlockSpec(memory_space=VMEM),
        compiler_params=pltpu.CompilerParams(vmem_limit_bytes=6 * 2**20),
        name="join_cores",
    )(partial, comb, other)


def split_kernel(rows_ref, mine_ref, other_ref):
    me = core_index()
    mine_ref[...] = rows_ref[:, me]
    other_ref[...] = rows_ref[:, 1 - me]


def split_cores(rows):
    slots, _, count, columns = rows.shape
    return pl.pallas_call(
        split_kernel,
        out_shape=[VMEM((slots, count, columns), rows.dtype)] * 2,
        in_specs=[pl.BlockSpec(memory_space=VMEM)],
        out_specs=[pl.BlockSpec(memory_space=VMEM)] * 2,
        compiler_params=pltpu.CompilerParams(vmem_limit_bytes=6 * 2**20),
        name="split_cores",
    )(rows)


def inverse_roots(factors):
    fifth = [1.25 ** (5 - k) * (-0.25) ** k * c for k, c in enumerate((1, 5, 10, 10, 5, 1))]
    coefficients = [1.5625, -0.3125, 0.0, 0.0, 0.0, 0.0, 0.0]
    for k, value in enumerate(fifth):
        coefficients[k + 1] -= value / 4
    order = factors[0].shape[0]
    rows = lax.broadcasted_iota(jnp.int32, (order, order), 0)
    cols = lax.broadcasted_iota(jnp.int32, (order, order), 1)
    norms = [jnp.sqrt(jnp.sum(factor * factor, keepdims=True)) for factor in factors]
    scalings = [2.5 / norm for norm in norms]
    once = [factor * scaling for factor, scaling in zip(factors, scalings)]
    twice = [bf16_dot(m, m) for m in once]
    thrice = [bf16_dot(m2, m) for m2, m in zip(twice, once)]
    p = coefficients
    roots = []
    for m, m2, m3, scaling in zip(once, twice, thrice, scalings):
        low = p[1] * m + p[2] * m2 + p[3] * m3
        high = p[4] * m + p[5] * m2 + p[6] * m3
        total = bf16_dot(high, m3) + low
        total = jnp.where(rows == cols, total + p[0], total)
        roots.append(total * jnp.sqrt(jnp.sqrt(scaling)))
    return roots


def refreshing(refresh_ref):
    mine = lax.axis_index("dp") * lax.axis_size("fsdp") + lax.axis_index("fsdp")
    return lax.rem(mine, REFRESH_PERIOD) == refresh_ref[0]


def load_kernel(tie_ref, *refs):
    del tie_ref
    count = len(refs) // 2
    loads = [
        pltpu.make_async_copy(refs[i], refs[count + i], refs[-1].at[i]) for i in range(count)
    ]
    for load in loads:
        load.start()
    for load in loads:
        load.wait()


def load_matrices(tie, *matrices):
    return pl.pallas_call(
        load_kernel,
        out_shape=[VMEM(m.shape, m.dtype) for m in matrices],
        in_specs=[pl.BlockSpec(memory_space=pl.ANY)] + [pl.BlockSpec(memory_space=HBM)] * len(matrices),
        out_specs=[pl.BlockSpec(memory_space=VMEM)] * len(matrices),
        scratch_shapes=[pltpu.SemaphoreType.DMA((len(matrices),))],
        compiler_params=pltpu.CompilerParams(vmem_limit_bytes=8 * 2**20),
        name="load_matrices",
    )(tie, *[pltpu.with_memory_space_constraint(m, HBM) for m in matrices])


def gram_rows(grad):
    return bf16_dot(grad, grad, ((1,), (1,))) * (1.0 / grad.shape[0])


def gram_columns(grad):
    return bf16_dot(grad, grad, ((0,), (0,))) * (1.0 / grad.shape[0])


def update_kernel(
    refresh_ref, grad_ref, left_ref, right_ref, lroot_ref, rroot_ref,
    new_lroot_ref, new_rroot_ref, update_ref, roots, sems,
):
    grad = grad_ref[...]
    refreshed = refreshing(refresh_ref)

    @pl.when(refreshed)
    def _():
        new_left = left_ref[...] + gram_rows(grad)
        new_right = right_ref[...] + gram_columns(grad)
        new_roots = inverse_roots((new_left, new_right))
        writes = []
        for i, (root, out_ref) in enumerate(zip(new_roots, (new_lroot_ref, new_rroot_ref))):
            roots[i] = root
            write = pltpu.make_async_copy(roots.at[i], out_ref, sems.at[i])
            write.start()
            writes.append(write)
        mixed = bf16_dot(roots[0], grad)
        update_ref[...] = bf16_dot(mixed, roots[1]).astype(update_ref.dtype)
        for write in writes:
            write.wait()

    @pl.when(jnp.logical_not(refreshed))
    def _():
        loads = [
            pltpu.make_async_copy(source, roots.at[i], sems.at[i])
            for i, source in enumerate((lroot_ref, rroot_ref))
        ]
        for load in loads:
            load.start()
        loads[0].wait()
        mixed = bf16_dot(roots[0], grad)
        loads[1].wait()
        update_ref[...] = bf16_dot(mixed, roots[1]).astype(update_ref.dtype)


def owner_update(refresh, grad, left, right, lroot, rroot):
    order = grad.shape[0]
    return pl.pallas_call(
        update_kernel,
        out_shape=(
            HBM((order, order), jnp.float32),
            HBM((order, order), jnp.float32),
            VMEM((order, order), jnp.bfloat16),
        ),
        in_specs=[pl.BlockSpec(memory_space=SMEM)]
        + [pl.BlockSpec(memory_space=VMEM)] * 3
        + [pl.BlockSpec(memory_space=HBM)] * 2,
        out_specs=(pl.BlockSpec(memory_space=HBM),) * 2 + (pl.BlockSpec(memory_space=VMEM),),
        scratch_shapes=[
            pltpu.VMEM((2, order, order), jnp.float32),
            pltpu.SemaphoreType.DMA((2,)),
        ],
        compiler_params=pltpu.CompilerParams(vmem_limit_bytes=24 * 2**20),
        name="owner_update",
    )(refresh, grad, left, right, lroot, rroot)


def factors_kernel(
    tie_ref, refresh_ref, grad_ref, left_ref, right_ref, lroot_ref, rroot_ref, old_l_ref, old_r_ref,
    new_left_ref, new_right_ref, new_lroot_ref, new_rroot_ref,
    left, right, roots, sems,
):
    del tie_ref, old_l_ref, old_r_ref
    kept = jnp.logical_not(refreshing(refresh_ref))
    loads = [
        pltpu.make_async_copy(source, roots.at[i], sems.at[2 + i])
        for i, source in enumerate((lroot_ref, rroot_ref))
    ]
    keeps = [
        pltpu.make_async_copy(roots.at[i], target, sems.at[2 + i])
        for i, target in enumerate((new_lroot_ref, new_rroot_ref))
    ]

    @pl.when(kept)
    def _():
        for load in loads:
            load.start()

    grad = grad_ref[...]
    left[...] = left_ref[...] + gram_rows(grad)
    write_left = pltpu.make_async_copy(left, new_left_ref, sems.at[0])
    write_left.start()
    right[...] = right_ref[...] + gram_columns(grad)
    write_right = pltpu.make_async_copy(right, new_right_ref, sems.at[1])
    write_right.start()

    @pl.when(kept)
    def _():
        for load, keep in zip(loads, keeps, strict=True):
            load.wait()
            keep.start()
        for keep in keeps:
            keep.wait()

    write_left.wait()
    write_right.wait()


def owner_factors(tie, refresh, grad, left, right, lroot, rroot, new_lroot, new_rroot):
    order = grad.shape[0]
    return pl.pallas_call(
        factors_kernel,
        out_shape=(HBM((order, order), jnp.float32),) * 4,
        in_specs=[pl.BlockSpec(memory_space=pl.ANY), pl.BlockSpec(memory_space=SMEM)]
        + [pl.BlockSpec(memory_space=VMEM)] * 3
        + [pl.BlockSpec(memory_space=HBM)] * 4,
        out_specs=(pl.BlockSpec(memory_space=HBM),) * 4,
        scratch_shapes=[pltpu.VMEM((order, order), jnp.float32)] * 2
        + [pltpu.VMEM((2, order, order), jnp.float32), pltpu.SemaphoreType.DMA((4,))],
        input_output_aliases={7: 2, 8: 3},
        compiler_params=pltpu.CompilerParams(vmem_limit_bytes=16 * 2**20),
        name="owner_factors",
    )(
        tie,
        refresh,
        grad, left, right, lroot, rroot, new_lroot, new_rroot,
    )


def per_device(grads, left_factor, right_factor, left_root, right_root, block_of_slot, refresh):
    shard_count = lax.axis_size("fsdp")
    local = grads[0]
    blocks, piece_rows, order = local.shape
    chips = shard_count // 2

    def to_next(piece):
        return lax.ppermute(piece, "dp", [(i, (i + 1) % N_DP) for i in range(N_DP)])

    def to_prev(piece):
        return lax.ppermute(piece, "dp", [(i, (i - 1) % N_DP) for i in range(N_DP)])

    def to_core(piece):
        return lax.ppermute(piece, "fsdp", [(i, i ^ 1) for i in range(shard_count)])

    def over_chips(rows):
        groups = [list(range(core, shard_count, 2)) for core in range(2)]
        return lax.all_to_all(
            rows, "fsdp", split_axis=0, concat_axis=0, axis_index_groups=groups, tiled=True
        )

    held, index, relay_b, relay_a = order_first(block_of_slot, local, ((2, 1), (2, 0)))
    relayed_b, relayed_a = to_prev(relay_b), to_next(relay_a)
    refresh, raw_b, raw_a, own_b, own_a, mine_b, mine_a = order_rest(
        index, refresh, held, ((1, 1), (3, 0), (3, 1), (1, 0), (0, 1), (0, 0))
    )
    raw_b, raw_a = to_next(raw_b), to_prev(raw_a)
    sum_b = add_pieces(own_b, relayed_b, own_b.dtype, "add_relay")
    sum_a = add_pieces(own_a, relayed_a, own_a.dtype, "add_relay")
    comb_b, comb_a = to_prev(sum_b), to_next(sum_a)
    left, right = load_matrices(sum_a, left_factor[0], right_factor[0])
    lroot, rroot = (
        pltpu.with_memory_space_constraint(root[0], HBM) for root in (left_root, right_root)
    )
    partial_b = add_pieces(mine_b, raw_b, jnp.float32, "add_raw", left)
    partial_a = add_pieces(mine_a, raw_a, jnp.float32, "add_raw")
    other = to_core(add_pieces(partial_b, comb_b, comb_b.dtype, "add_comb"))
    grad = over_chips(join_cores(partial_a, comb_a, other)).reshape(order, order)

    new_lroot, new_rroot, update = owner_update(refresh, grad, left, right, lroot, rroot)

    rows = over_chips(update.reshape(chips, 2, piece_rows, order))
    rows_a, other = split_cores(rows)
    prev_a = to_next(rows_a)
    rows_b = to_core(other)
    next_b = to_prev(rows_b)
    prev_b, next_a = to_next(rows_b), to_prev(rows_a)
    over_a, over_b = to_next(prev_a), to_prev(next_b)
    new_left, new_right, new_lroot, new_rroot = owner_factors(
        rows_a, refresh, grad, left, right, lroot, rroot, new_lroot, new_rroot
    )
    over_a, over_b = to_next(prev_a), to_prev(next_b)
    updates = place_blocks(
        index,
        (rows_a, rows_b, prev_a, next_b, prev_b, next_a),
        ((0, 0), (0, 1), (3, 0), (1, 1), (3, 1), (1, 0)),
        "place_early",
    )
    updates = place_blocks(index, (over_a,), ((2, 0),), "place_over", updates)
    updates = place_blocks(index, (over_b,), ((2, 1),), "place_last", updates)
    return new_left[None], new_right[None], new_lroot[None], new_rroot[None], updates


def solution(mesh):
    owned = P(("dp", "fsdp"), None, None)
    return jax.shard_map(
        per_device,
        mesh=mesh,
        in_specs=(P("dp", None, "fsdp", None), owned, owned, owned, owned, P(), P()),
        out_specs=(owned, owned, owned, owned, P(None, "fsdp", None)),
        check_vma=False,
    )
```

```python
import functools

import jax
import jax.numpy as jnp
from jax import lax
from jax.experimental import pallas as pl
from jax.experimental.pallas import tpu as pltpu
from jax.sharding import PartitionSpec as P

ITERS = 2
REFRESH_PERIOD = 16
N_DP = 4

VMEM = pltpu.VMEM
SMEM = pltpu.SMEM
HBM = pltpu.HBM


def bf16_dot(a, b, dims=((1,), (0,))):
    return lax.dot_general(
        a.astype(jnp.bfloat16),
        b.astype(jnp.bfloat16),
        (dims, ((), ())),
        preferred_element_type=jnp.float32,
    )


def core_index():
    return lax.rem(lax.axis_index("fsdp"), 2)


def piece_slots(quarter, parity, slots):
    start = lax.rem(lax.axis_index("dp") + quarter, N_DP) * (slots // N_DP)
    return start + lax.rem(core_index() + parity, 2)


def copy_rows(index_smem, source_ref, out_ref, start):
    def body(slot, carry):
        out_ref[slot] = source_ref[index_smem[start + 2 * slot]]
        return carry

    lax.fori_loop(0, out_ref.shape[0], body, 0, unroll=8)


CHUNKS = 8


def order_first_kernel(pieces, index_ref, source_ref, held_ref, index_smem, *refs):
    outs, (index_sem, sems) = refs[: len(pieces)], refs[len(pieces) :]
    fetch = pltpu.make_async_copy(index_ref, index_smem, index_sem)
    fetch.start()
    count = source_ref.shape[0] // CHUNKS
    loads = [
        pltpu.make_async_copy(
            source_ref.at[pl.ds(i * count, count)], held_ref.at[pl.ds(i * count, count)], sems.at[i]
        )
        for i in range(CHUNKS)
    ]
    for load in loads:
        load.start()
    fetch.wait()
    for load in loads:
        load.wait()
    for (quarter, parity), out_ref in zip(pieces, outs, strict=True):
        copy_rows(index_smem, held_ref, out_ref, piece_slots(quarter, parity, index_ref.shape[0]))


def order_rest_kernel(pieces, index_ref, refresh_ref, held_ref, refresh_smem, *outs):
    refresh_smem[0] = refresh_ref[0]
    for (quarter, parity), out_ref in zip(pieces, outs, strict=True):
        copy_rows(index_ref, held_ref, out_ref, piece_slots(quarter, parity, index_ref.shape[0]))


def order_first(index, source, pieces):
    piece = (source.shape[0] // N_DP // 2, *source.shape[1:])
    return pl.pallas_call(
        functools.partial(order_first_kernel, pieces),
        out_shape=[VMEM(source.shape, source.dtype), SMEM(index.shape, index.dtype)]
        + [VMEM(piece, source.dtype) for _ in pieces],
        in_specs=[pl.BlockSpec(memory_space=HBM)] * 2,
        out_specs=[pl.BlockSpec(memory_space=VMEM), pl.BlockSpec(memory_space=SMEM)]
        + [pl.BlockSpec(memory_space=VMEM)] * len(pieces),
        scratch_shapes=[pltpu.SemaphoreType.DMA, pltpu.SemaphoreType.DMA((CHUNKS,))],
        compiler_params=pltpu.CompilerParams(vmem_limit_bytes=8 * 2**20),
        name="order_first",
    )(
        pltpu.with_memory_space_constraint(index, HBM),
        pltpu.with_memory_space_constraint(source, HBM),
    )


def order_rest(index, refresh, held, pieces):
    piece = (held.shape[0] // N_DP // 2, *held.shape[1:])
    return pl.pallas_call(
        functools.partial(order_rest_kernel, pieces),
        out_shape=[SMEM(refresh.shape, refresh.dtype)]
        + [VMEM(piece, held.dtype) for _ in pieces],
        in_specs=[pl.BlockSpec(memory_space=space) for space in (SMEM, SMEM, VMEM)],
        out_specs=[pl.BlockSpec(memory_space=SMEM)]
        + [pl.BlockSpec(memory_space=VMEM)] * len(pieces),
        compiler_params=pltpu.CompilerParams(vmem_limit_bytes=8 * 2**20),
        name="order_rest",
    )(index, refresh, held)


def place_kernel(pieces, aliased, index_ref, *refs):
    sources = refs[: len(pieces)]
    out_ref, sems = refs[len(pieces) + aliased :]
    for number, ((quarter, parity), source_ref) in enumerate(zip(pieces, sources, strict=True)):
        start = piece_slots(quarter, parity, index_ref.shape[0])

        def body(slot, carry, source_ref=source_ref, number=number, start=start):
            pltpu.make_async_copy(
                source_ref.at[slot], out_ref.at[index_ref[start + 2 * slot]], sems.at[number]
            ).start()
            return carry

        lax.fori_loop(0, source_ref.shape[0], body, 0, unroll=16)
    for number, source_ref in enumerate(sources):
        pltpu.make_async_copy(source_ref, source_ref, sems.at[number]).wait()


def place_blocks(index, sources, pieces, name, out=None):
    rows, columns = sources[0].shape[1:]
    aliased = 0 if out is None else 1
    return pl.pallas_call(
        functools.partial(place_kernel, pieces, aliased),
        out_shape=jax.ShapeDtypeStruct((index.shape[0], rows, columns), sources[0].dtype),
        in_specs=[pl.BlockSpec(memory_space=SMEM)]
        + [pl.BlockSpec(memory_space=pl.ANY)] * (len(sources) + aliased),
        out_specs=pl.BlockSpec(memory_space=pl.ANY),
        scratch_shapes=[pltpu.SemaphoreType.DMA((len(pieces),))],
        input_output_aliases={1 + len(sources): 0} if aliased else {},
        compiler_params=pltpu.CompilerParams(vmem_limit_bytes=4 * 2**20),
        cost_estimate=pl.CostEstimate(
            flops=0, bytes_accessed=64 * rows * columns * 64 * len(sources), transcendentals=0
        ),
        name=name,
    )(index, *sources, *(() if out is None else (out,)))


def add_kernel(*refs):
    total = refs[0][...].astype(jnp.float32) + refs[1][...].astype(jnp.float32)
    refs[-1][...] = total.astype(refs[-1].dtype)


def add_pieces(first, second, dtype, name, tie=None):
    ties = () if tie is None else (tie,)
    return pl.pallas_call(
        add_kernel,
        out_shape=VMEM(first.shape, dtype),
        in_specs=[pl.BlockSpec(memory_space=VMEM)] * 2
        + [pl.BlockSpec(memory_space=pl.ANY)] * len(ties),
        out_specs=pl.BlockSpec(memory_space=VMEM),
        compiler_params=pltpu.CompilerParams(vmem_limit_bytes=6 * 2**20),
        name=name,
    )(first, second, *ties)


def join_kernel(partial_ref, comb_ref, other_ref, out_ref):
    me = core_index()
    total = partial_ref[...] + comb_ref[...].astype(jnp.float32)
    out_ref[:, me] = total.astype(out_ref.dtype)
    out_ref[:, 1 - me] = other_ref[...]


def join_cores(partial, comb, other):
    slots, rows, columns = comb.shape
    return pl.pallas_call(
        join_kernel,
        out_shape=VMEM((slots, 2, rows, columns), comb.dtype),
        in_specs=[pl.BlockSpec(memory_space=VMEM)] * 3,
        out_specs=pl.BlockSpec(memory_space=VMEM),
        compiler_params=pltpu.CompilerParams(vmem_limit_bytes=6 * 2**20),
        name="join_cores",
    )(partial, comb, other)


def split_kernel(rows_ref, mine_ref, other_ref):
    me = core_index()
    mine_ref[...] = rows_ref[:, me]
    other_ref[...] = rows_ref[:, 1 - me]


def split_cores(rows):
    slots, _, count, columns = rows.shape
    return pl.pallas_call(
        split_kernel,
        out_shape=[VMEM((slots, count, columns), rows.dtype)] * 2,
        in_specs=[pl.BlockSpec(memory_space=VMEM)],
        out_specs=[pl.BlockSpec(memory_space=VMEM)] * 2,
        compiler_params=pltpu.CompilerParams(vmem_limit_bytes=6 * 2**20),
        name="split_cores",
    )(rows)


def inverse_roots(factors):
    fifth = [1.25 ** (5 - k) * (-0.25) ** k * c for k, c in enumerate((1, 5, 10, 10, 5, 1))]
    coefficients = [1.5625, -0.3125, 0.0, 0.0, 0.0, 0.0, 0.0]
    for k, value in enumerate(fifth):
        coefficients[k + 1] -= value / 4
    order = factors[0].shape[0]
    rows = lax.broadcasted_iota(jnp.int32, (order, order), 0)
    cols = lax.broadcasted_iota(jnp.int32, (order, order), 1)
    norms = [jnp.sqrt(jnp.sum(factor * factor, keepdims=True)) for factor in factors]
    scalings = [2.5 / norm for norm in norms]
    once = [factor * scaling for factor, scaling in zip(factors, scalings)]
    twice = [bf16_dot(m, m) for m in once]
    thrice = [bf16_dot(m2, m) for m2, m in zip(twice, once)]
    p = coefficients
    roots = []
    for m, m2, m3, scaling in zip(once, twice, thrice, scalings):
        low = p[1] * m + p[2] * m2 + p[3] * m3
        high = p[4] * m + p[5] * m2 + p[6] * m3
        total = bf16_dot(high, m3) + low
        total = jnp.where(rows == cols, total + p[0], total)
        roots.append(total * jnp.sqrt(jnp.sqrt(scaling)))
    return roots


def refreshing(refresh_ref):
    mine = lax.axis_index("dp") * lax.axis_size("fsdp") + lax.axis_index("fsdp")
    return lax.rem(mine, REFRESH_PERIOD) == refresh_ref[0]


def load_kernel(tie_ref, *refs):
    del tie_ref
    count = len(refs) // 2
    loads = [
        pltpu.make_async_copy(refs[i], refs[count + i], refs[-1].at[i]) for i in range(count)
    ]
    for load in loads:
        load.start()
    for load in loads:
        load.wait()


def load_matrices(tie, *matrices):
    return pl.pallas_call(
        load_kernel,
        out_shape=[VMEM(m.shape, m.dtype) for m in matrices],
        in_specs=[pl.BlockSpec(memory_space=pl.ANY)] + [pl.BlockSpec(memory_space=HBM)] * len(matrices),
        out_specs=[pl.BlockSpec(memory_space=VMEM)] * len(matrices),
        scratch_shapes=[pltpu.SemaphoreType.DMA((len(matrices),))],
        compiler_params=pltpu.CompilerParams(vmem_limit_bytes=8 * 2**20),
        name="load_matrices",
    )(tie, *[pltpu.with_memory_space_constraint(m, HBM) for m in matrices])


def gram_rows(grad):
    return bf16_dot(grad, grad, ((1,), (1,))) * (1.0 / grad.shape[0])


def gram_columns(grad):
    return bf16_dot(grad, grad, ((0,), (0,))) * (1.0 / grad.shape[0])


def update_kernel(
    refresh_ref, grad_ref, left_ref, right_ref, lroot_ref, rroot_ref, update_ref, roots, sems
):
    grad = grad_ref[...]
    refreshed = refreshing(refresh_ref)

    @pl.when(refreshed)
    def _():
        new_left = left_ref[...] + gram_rows(grad)
        new_right = right_ref[...] + gram_columns(grad)
        new_lroot, new_rroot = inverse_roots((new_left, new_right))
        mixed = bf16_dot(new_lroot, grad)
        update_ref[...] = bf16_dot(mixed, new_rroot).astype(update_ref.dtype)

    @pl.when(jnp.logical_not(refreshed))
    def _():
        loads = [
            pltpu.make_async_copy(source, roots.at[i], sems.at[i])
            for i, source in enumerate((lroot_ref, rroot_ref))
        ]
        for load in loads:
            load.start()
        loads[0].wait()
        mixed = bf16_dot(roots[0], grad)
        loads[1].wait()
        update_ref[...] = bf16_dot(mixed, roots[1]).astype(update_ref.dtype)


def owner_update(refresh, grad, left, right, lroot, rroot):
    order = grad.shape[0]
    return pl.pallas_call(
        update_kernel,
        out_shape=VMEM((order, order), jnp.bfloat16),
        in_specs=[pl.BlockSpec(memory_space=SMEM)]
        + [pl.BlockSpec(memory_space=VMEM)] * 3
        + [pl.BlockSpec(memory_space=HBM)] * 2,
        out_specs=pl.BlockSpec(memory_space=VMEM),
        scratch_shapes=[
            pltpu.VMEM((2, order, order), jnp.float32),
            pltpu.SemaphoreType.DMA((2,)),
        ],
        compiler_params=pltpu.CompilerParams(vmem_limit_bytes=24 * 2**20),
        name="owner_update",
    )(refresh, grad, left, right, lroot, rroot)


def factors_kernel(
    tie_ref, refresh_ref, grad_ref, left_ref, right_ref, lroot_ref, rroot_ref,
    new_left_ref, new_right_ref, new_lroot_ref, new_rroot_ref, factors, roots, sems,
):
    del tie_ref
    refreshed = refreshing(refresh_ref)
    loads = [
        pltpu.make_async_copy(source, roots.at[i], sems.at[2 + i])
        for i, source in enumerate((lroot_ref, rroot_ref))
    ]
    targets = (new_left_ref, new_right_ref)
    writes = [pltpu.make_async_copy(factors.at[i], t, sems.at[i]) for i, t in enumerate(targets)]
    targets = (new_lroot_ref, new_rroot_ref)
    writes += [pltpu.make_async_copy(roots.at[i], t, sems.at[2 + i]) for i, t in enumerate(targets)]
    for load in loads:
        load.start()
    grad = grad_ref[...]
    factors[0] = left_ref[...] + gram_rows(grad)
    writes[0].start()
    factors[1] = right_ref[...] + gram_columns(grad)
    writes[1].start()
    for load in loads:
        load.wait()

    @pl.when(refreshed)
    def _():
        roots[0], roots[1] = inverse_roots((factors[0], factors[1]))

    for write in writes[2:]:
        write.start()
    for write in writes:
        write.wait()


def owner_factors(tie, refresh, grad, left, right, lroot, rroot):
    order = grad.shape[0]
    return pl.pallas_call(
        factors_kernel,
        out_shape=(HBM((order, order), jnp.float32),) * 4,
        in_specs=[pl.BlockSpec(memory_space=pl.ANY), pl.BlockSpec(memory_space=SMEM)]
        + [pl.BlockSpec(memory_space=VMEM)] * 3
        + [pl.BlockSpec(memory_space=HBM)] * 2,
        out_specs=(pl.BlockSpec(memory_space=HBM),) * 4,
        scratch_shapes=[pltpu.VMEM((2, order, order), jnp.float32)] * 2
        + [pltpu.SemaphoreType.DMA((4,))],
        compiler_params=pltpu.CompilerParams(vmem_limit_bytes=24 * 2**20),
        name="owner_factors",
    )(tie, refresh, grad, left, right, lroot, rroot)


def per_device(grads, left_factor, right_factor, left_root, right_root, block_of_slot, refresh):
    shard_count = lax.axis_size("fsdp")
    local = grads[0]
    blocks, piece_rows, order = local.shape
    chips = shard_count // 2

    def to_next(piece):
        return lax.ppermute(piece, "dp", [(i, (i + 1) % N_DP) for i in range(N_DP)])

    def to_prev(piece):
        return lax.ppermute(piece, "dp", [(i, (i - 1) % N_DP) for i in range(N_DP)])

    def to_core(piece):
        return lax.ppermute(piece, "fsdp", [(i, i ^ 1) for i in range(shard_count)])

    def over_chips(rows):
        groups = [list(range(core, shard_count, 2)) for core in range(2)]
        return lax.all_to_all(
            rows, "fsdp", split_axis=0, concat_axis=0, axis_index_groups=groups, tiled=True
        )

    held, index, relay_b, relay_a = order_first(block_of_slot, local, ((2, 1), (2, 0)))
    relayed_b, relayed_a = to_prev(relay_b), to_next(relay_a)
    refresh, raw_b, raw_a, own_b, own_a, mine_b, mine_a = order_rest(
        index, refresh, held, ((1, 1), (3, 0), (3, 1), (1, 0), (0, 1), (0, 0))
    )
    raw_b, raw_a = to_next(raw_b), to_prev(raw_a)
    sum_b = add_pieces(own_b, relayed_b, own_b.dtype, "add_relay")
    sum_a = add_pieces(own_a, relayed_a, own_a.dtype, "add_relay")
    comb_b, comb_a = to_prev(sum_b), to_next(sum_a)
    left, right = load_matrices(sum_a, left_factor[0], right_factor[0])
    lroot, rroot = (
        pltpu.with_memory_space_constraint(root[0], HBM) for root in (left_root, right_root)
    )
    partial_b = add_pieces(mine_b, raw_b, jnp.float32, "add_raw", left)
    partial_a = add_pieces(mine_a, raw_a, jnp.float32, "add_raw")
    other = to_core(add_pieces(partial_b, comb_b, comb_b.dtype, "add_comb"))
    grad = over_chips(join_cores(partial_a, comb_a, other)).reshape(order, order)

    update = owner_update(refresh, grad, left, right, lroot, rroot)

    rows = over_chips(update.reshape(chips, 2, piece_rows, order))
    rows_a, other = split_cores(rows)
    prev_a = to_next(rows_a)
    rows_b = to_core(other)
    next_b = to_prev(rows_b)
    prev_b, next_a = to_next(rows_b), to_prev(rows_a)
    over_a, over_b = to_next(prev_a), to_prev(next_b)
    new_left, new_right, new_lroot, new_rroot = owner_factors(
        rows_a, refresh, grad, left, right, lroot, rroot
    )
    over_a, over_b = to_next(prev_a), to_prev(next_b)
    updates = place_blocks(
        index,
        (rows_a, rows_b, prev_a, next_b, prev_b, next_a),
        ((0, 0), (0, 1), (3, 0), (1, 1), (3, 1), (1, 0)),
        "place_early",
    )
    updates = place_blocks(index, (over_a,), ((2, 0),), "place_over", updates)
    updates = place_blocks(index, (over_b,), ((2, 1),), "place_last", updates)
    return new_left[None], new_right[None], new_lroot[None], new_rroot[None], updates


def solution(mesh):
    owned = P(("dp", "fsdp"), None, None)
    return jax.shard_map(
        per_device,
        mesh=mesh,
        in_specs=(P("dp", None, "fsdp", None), owned, owned, owned, owned, P(), P()),
        out_specs=(owned, owned, owned, owned, P(None, "fsdp", None)),
        check_vma=False,
    )
```

```python
import functools

import jax
import jax.numpy as jnp
from jax import lax
from jax.experimental import pallas as pl
from jax.experimental.pallas import tpu as pltpu
from jax.sharding import PartitionSpec as P

ITERS = 2
REFRESH_PERIOD = 16
N_DP = 4

VMEM = pltpu.VMEM
SMEM = pltpu.SMEM
HBM = pltpu.HBM


def bf16_dot(a, b, dims=((1,), (0,))):
    return lax.dot_general(
        a.astype(jnp.bfloat16),
        b.astype(jnp.bfloat16),
        (dims, ((), ())),
        preferred_element_type=jnp.float32,
    )


def core_index():
    return lax.rem(lax.axis_index("fsdp"), 2)


def piece_slots(quarter, parity, slots):
    start = lax.rem(lax.axis_index("dp") + quarter, N_DP) * (slots // N_DP)
    return start + lax.rem(core_index() + parity, 2)


def copy_rows(index_smem, source_ref, out_ref, start):
    def body(slot, carry):
        out_ref[slot] = source_ref[index_smem[start + 2 * slot]]
        return carry

    lax.fori_loop(0, out_ref.shape[0], body, 0, unroll=8)


CHUNKS = 8


def order_first_kernel(pieces, index_ref, source_ref, held_ref, index_smem, *refs):
    outs, (index_sem, sems) = refs[: len(pieces)], refs[len(pieces) :]
    fetch = pltpu.make_async_copy(index_ref, index_smem, index_sem)
    fetch.start()
    count = source_ref.shape[0] // CHUNKS
    loads = [
        pltpu.make_async_copy(
            source_ref.at[pl.ds(i * count, count)], held_ref.at[pl.ds(i * count, count)], sems.at[i]
        )
        for i in range(CHUNKS)
    ]
    for load in loads:
        load.start()
    fetch.wait()
    for load in loads:
        load.wait()
    for (quarter, parity), out_ref in zip(pieces, outs, strict=True):
        copy_rows(index_smem, held_ref, out_ref, piece_slots(quarter, parity, index_ref.shape[0]))


def order_rest_kernel(pieces, index_ref, refresh_ref, held_ref, refresh_smem, *outs):
    refresh_smem[0] = refresh_ref[0]
    for (quarter, parity), out_ref in zip(pieces, outs, strict=True):
        copy_rows(index_ref, held_ref, out_ref, piece_slots(quarter, parity, index_ref.shape[0]))


def order_first(index, source, pieces):
    piece = (source.shape[0] // N_DP // 2, *source.shape[1:])
    return pl.pallas_call(
        functools.partial(order_first_kernel, pieces),
        out_shape=[VMEM(source.shape, source.dtype), SMEM(index.shape, index.dtype)]
        + [VMEM(piece, source.dtype) for _ in pieces],
        in_specs=[pl.BlockSpec(memory_space=HBM)] * 2,
        out_specs=[pl.BlockSpec(memory_space=VMEM), pl.BlockSpec(memory_space=SMEM)]
        + [pl.BlockSpec(memory_space=VMEM)] * len(pieces),
        scratch_shapes=[pltpu.SemaphoreType.DMA, pltpu.SemaphoreType.DMA((CHUNKS,))],
        compiler_params=pltpu.CompilerParams(vmem_limit_bytes=8 * 2**20),
        name="order_first",
    )(
        pltpu.with_memory_space_constraint(index, HBM),
        pltpu.with_memory_space_constraint(source, HBM),
    )


def order_rest(index, refresh, held, pieces):
    piece = (held.shape[0] // N_DP // 2, *held.shape[1:])
    return pl.pallas_call(
        functools.partial(order_rest_kernel, pieces),
        out_shape=[SMEM(refresh.shape, refresh.dtype)]
        + [VMEM(piece, held.dtype) for _ in pieces],
        in_specs=[pl.BlockSpec(memory_space=space) for space in (SMEM, SMEM, VMEM)],
        out_specs=[pl.BlockSpec(memory_space=SMEM)]
        + [pl.BlockSpec(memory_space=VMEM)] * len(pieces),
        compiler_params=pltpu.CompilerParams(vmem_limit_bytes=8 * 2**20),
        name="order_rest",
    )(index, refresh, held)


def place_kernel(pieces, aliased, index_ref, *refs):
    sources = refs[: len(pieces)]
    out_ref, sems = refs[len(pieces) + aliased :]
    for number, ((quarter, parity), source_ref) in enumerate(zip(pieces, sources, strict=True)):
        start = piece_slots(quarter, parity, index_ref.shape[0])

        def body(slot, carry, source_ref=source_ref, number=number, start=start):
            pltpu.make_async_copy(
                source_ref.at[slot], out_ref.at[index_ref[start + 2 * slot]], sems.at[number]
            ).start()
            return carry

        lax.fori_loop(0, source_ref.shape[0], body, 0, unroll=16)
    for number, source_ref in enumerate(sources):
        pltpu.make_async_copy(source_ref, source_ref, sems.at[number]).wait()


def place_blocks(index, sources, pieces, name, out=None):
    rows, columns = sources[0].shape[1:]
    aliased = 0 if out is None else 1
    return pl.pallas_call(
        functools.partial(place_kernel, pieces, aliased),
        out_shape=jax.ShapeDtypeStruct((index.shape[0], rows, columns), sources[0].dtype),
        in_specs=[pl.BlockSpec(memory_space=SMEM)]
        + [pl.BlockSpec(memory_space=pl.ANY)] * (len(sources) + aliased),
        out_specs=pl.BlockSpec(memory_space=pl.ANY),
        scratch_shapes=[pltpu.SemaphoreType.DMA((len(pieces),))],
        input_output_aliases={1 + len(sources): 0} if aliased else {},
        compiler_params=pltpu.CompilerParams(vmem_limit_bytes=4 * 2**20),
        cost_estimate=pl.CostEstimate(
            flops=0, bytes_accessed=64 * rows * columns * 64 * len(sources), transcendentals=0
        ),
        name=name,
    )(index, *sources, *(() if out is None else (out,)))


def add_kernel(*refs):
    total = refs[0][...].astype(jnp.float32) + refs[1][...].astype(jnp.float32)
    refs[-1][...] = total.astype(refs[-1].dtype)


def add_pieces(first, second, dtype, name, tie=None):
    ties = () if tie is None else (tie,)
    return pl.pallas_call(
        add_kernel,
        out_shape=VMEM(first.shape, dtype),
        in_specs=[pl.BlockSpec(memory_space=VMEM)] * 2
        + [pl.BlockSpec(memory_space=pl.ANY)] * len(ties),
        out_specs=pl.BlockSpec(memory_space=VMEM),
        compiler_params=pltpu.CompilerParams(vmem_limit_bytes=6 * 2**20),
        name=name,
    )(first, second, *ties)


def join_kernel(partial_ref, comb_ref, other_ref, out_ref):
    me = core_index()
    total = partial_ref[...] + comb_ref[...].astype(jnp.float32)
    out_ref[:, me] = total.astype(out_ref.dtype)
    out_ref[:, 1 - me] = other_ref[...]


def join_cores(partial, comb, other):
    slots, rows, columns = comb.shape
    return pl.pallas_call(
        join_kernel,
        out_shape=VMEM((slots, 2, rows, columns), comb.dtype),
        in_specs=[pl.BlockSpec(memory_space=VMEM)] * 3,
        out_specs=pl.BlockSpec(memory_space=VMEM),
        compiler_params=pltpu.CompilerParams(vmem_limit_bytes=6 * 2**20),
        name="join_cores",
    )(partial, comb, other)


def pick_kernel(core, rows_ref, tie_ref, out_ref):
    del tie_ref
    out_ref[...] = rows_ref[:, lax.rem(core_index() + core, 2)]


def pick_core(rows, core, tie):
    slots, _, count, columns = rows.shape
    return pl.pallas_call(
        functools.partial(pick_kernel, core),
        out_shape=VMEM((slots, count, columns), rows.dtype),
        in_specs=[pl.BlockSpec(memory_space=VMEM), pl.BlockSpec(memory_space=pl.ANY)],
        out_specs=pl.BlockSpec(memory_space=VMEM),
        compiler_params=pltpu.CompilerParams(vmem_limit_bytes=6 * 2**20),
        name="pick_core",
    )(rows, tie)


def inverse_roots(factors):
    fifth = [1.25 ** (5 - k) * (-0.25) ** k * c for k, c in enumerate((1, 5, 10, 10, 5, 1))]
    coefficients = [1.5625, -0.3125, 0.0, 0.0, 0.0, 0.0, 0.0]
    for k, value in enumerate(fifth):
        coefficients[k + 1] -= value / 4
    order = factors[0].shape[0]
    rows = lax.broadcasted_iota(jnp.int32, (order, order), 0)
    cols = lax.broadcasted_iota(jnp.int32, (order, order), 1)
    norms = [jnp.sqrt(jnp.sum(factor * factor, keepdims=True)) for factor in factors]
    scalings = [2.5 / norm for norm in norms]
    once = [factor * scaling for factor, scaling in zip(factors, scalings)]
    twice = [bf16_dot(m, m) for m in once]
    thrice = [bf16_dot(m2, m) for m2, m in zip(twice, once)]
    p = coefficients
    roots = []
    for m, m2, m3, scaling in zip(once, twice, thrice, scalings):
        low = p[1] * m + p[2] * m2 + p[3] * m3
        high = p[4] * m + p[5] * m2 + p[6] * m3
        total = bf16_dot(high, m3) + low
        total = jnp.where(rows == cols, total + p[0], total)
        roots.append(total * jnp.sqrt(jnp.sqrt(scaling)))
    return roots


def refreshing(refresh_ref):
    mine = lax.axis_index("dp") * lax.axis_size("fsdp") + lax.axis_index("fsdp")
    return lax.rem(mine, REFRESH_PERIOD) == refresh_ref[0]


def load_kernel(tie_ref, *refs):
    del tie_ref
    count = len(refs) // 2
    loads = [
        pltpu.make_async_copy(refs[i], refs[count + i], refs[-1].at[i]) for i in range(count)
    ]
    for load in loads:
        load.start()
    for load in loads:
        load.wait()


def load_matrices(tie, *matrices):
    return pl.pallas_call(
        load_kernel,
        out_shape=[VMEM(m.shape, m.dtype) for m in matrices],
        in_specs=[pl.BlockSpec(memory_space=pl.ANY)] + [pl.BlockSpec(memory_space=HBM)] * len(matrices),
        out_specs=[pl.BlockSpec(memory_space=VMEM)] * len(matrices),
        scratch_shapes=[pltpu.SemaphoreType.DMA((len(matrices),))],
        compiler_params=pltpu.CompilerParams(vmem_limit_bytes=8 * 2**20),
        name="load_matrices",
    )(tie, *[pltpu.with_memory_space_constraint(m, HBM) for m in matrices])


def gram_rows(grad):
    return bf16_dot(grad, grad, ((1,), (1,))) * (1.0 / grad.shape[0])


def gram_columns(grad):
    return bf16_dot(grad, grad, ((0,), (0,))) * (1.0 / grad.shape[0])


def update_kernel(
    refresh_ref, grad_ref, left_ref, right_ref, lroot_ref, rroot_ref, update_ref, roots, sems
):
    grad = grad_ref[...]
    refreshed = refreshing(refresh_ref)

    @pl.when(refreshed)
    def _():
        new_left = left_ref[...] + gram_rows(grad)
        new_right = right_ref[...] + gram_columns(grad)
        new_lroot, new_rroot = inverse_roots((new_left, new_right))
        mixed = bf16_dot(new_lroot, grad)
        update_ref[...] = bf16_dot(mixed, new_rroot).astype(update_ref.dtype)

    @pl.when(jnp.logical_not(refreshed))
    def _():
        loads = [
            pltpu.make_async_copy(source, roots.at[i], sems.at[i])
            for i, source in enumerate((lroot_ref, rroot_ref))
        ]
        for load in loads:
            load.start()
        loads[0].wait()
        mixed = bf16_dot(roots[0], grad)
        loads[1].wait()
        update_ref[...] = bf16_dot(mixed, roots[1]).astype(update_ref.dtype)


def owner_update(refresh, grad, left, right, lroot, rroot):
    order = grad.shape[0]
    return pl.pallas_call(
        update_kernel,
        out_shape=VMEM((order, order), jnp.bfloat16),
        in_specs=[pl.BlockSpec(memory_space=SMEM)]
        + [pl.BlockSpec(memory_space=VMEM)] * 3
        + [pl.BlockSpec(memory_space=HBM)] * 2,
        out_specs=pl.BlockSpec(memory_space=VMEM),
        scratch_shapes=[
            pltpu.VMEM((2, order, order), jnp.float32),
            pltpu.SemaphoreType.DMA((2,)),
        ],
        compiler_params=pltpu.CompilerParams(vmem_limit_bytes=24 * 2**20),
        name="owner_update",
    )(refresh, grad, left, right, lroot, rroot)


def factors_kernel(
    tie_ref, refresh_ref, grad_ref, left_ref, right_ref, lroot_ref, rroot_ref,
    new_left_ref, new_right_ref, new_lroot_ref, new_rroot_ref, factors, roots, sems,
):
    del tie_ref
    refreshed = refreshing(refresh_ref)
    loads = [
        pltpu.make_async_copy(source, roots.at[i], sems.at[2 + i])
        for i, source in enumerate((lroot_ref, rroot_ref))
    ]
    targets = (new_left_ref, new_right_ref)
    writes = [pltpu.make_async_copy(factors.at[i], t, sems.at[i]) for i, t in enumerate(targets)]
    targets = (new_lroot_ref, new_rroot_ref)
    writes += [pltpu.make_async_copy(roots.at[i], t, sems.at[2 + i]) for i, t in enumerate(targets)]
    for load in loads:
        load.start()
    grad = grad_ref[...]
    factors[0] = left_ref[...] + gram_rows(grad)
    writes[0].start()
    factors[1] = right_ref[...] + gram_columns(grad)
    writes[1].start()
    for load in loads:
        load.wait()

    @pl.when(refreshed)
    def _():
        roots[0], roots[1] = inverse_roots((factors[0], factors[1]))

    for write in writes[2:]:
        write.start()
    for write in writes:
        write.wait()


def owner_factors(tie, refresh, grad, left, right, lroot, rroot):
    order = grad.shape[0]
    return pl.pallas_call(
        factors_kernel,
        out_shape=(HBM((order, order), jnp.float32),) * 4,
        in_specs=[pl.BlockSpec(memory_space=pl.ANY), pl.BlockSpec(memory_space=SMEM)]
        + [pl.BlockSpec(memory_space=VMEM)] * 3
        + [pl.BlockSpec(memory_space=HBM)] * 2,
        out_specs=(pl.BlockSpec(memory_space=HBM),) * 4,
        scratch_shapes=[pltpu.VMEM((2, order, order), jnp.float32)] * 2
        + [pltpu.SemaphoreType.DMA((4,))],
        compiler_params=pltpu.CompilerParams(vmem_limit_bytes=24 * 2**20),
        name="owner_factors",
    )(tie, refresh, grad, left, right, lroot, rroot)


def per_device(grads, left_factor, right_factor, left_root, right_root, block_of_slot, refresh):
    shard_count = lax.axis_size("fsdp")
    local = grads[0]
    blocks, piece_rows, order = local.shape
    chips = shard_count // 2

    def to_next(piece):
        return lax.ppermute(piece, "dp", [(i, (i + 1) % N_DP) for i in range(N_DP)])

    def to_prev(piece):
        return lax.ppermute(piece, "dp", [(i, (i - 1) % N_DP) for i in range(N_DP)])

    def to_core(piece):
        return lax.ppermute(piece, "fsdp", [(i, i ^ 1) for i in range(shard_count)])

    def over_chips(rows):
        groups = [list(range(core, shard_count, 2)) for core in range(2)]
        return lax.all_to_all(
            rows, "fsdp", split_axis=0, concat_axis=0, axis_index_groups=groups, tiled=True
        )

    held, index, relay_b, relay_a = order_first(block_of_slot, local, ((2, 1), (2, 0)))
    relayed_b, relayed_a = to_prev(relay_b), to_next(relay_a)
    refresh, raw_b, raw_a, own_b, own_a, mine_b, mine_a = order_rest(
        index, refresh, held, ((1, 1), (3, 0), (3, 1), (1, 0), (0, 1), (0, 0))
    )
    raw_b, raw_a = to_next(raw_b), to_prev(raw_a)
    sum_b = add_pieces(own_b, relayed_b, own_b.dtype, "add_relay")
    sum_a = add_pieces(own_a, relayed_a, own_a.dtype, "add_relay")
    comb_b, comb_a = to_prev(sum_b), to_next(sum_a)
    left, right = load_matrices(sum_a, left_factor[0], right_factor[0])
    lroot, rroot = (
        pltpu.with_memory_space_constraint(root[0], HBM) for root in (left_root, right_root)
    )
    partial_b = add_pieces(mine_b, raw_b, jnp.float32, "add_raw", left)
    partial_a = add_pieces(mine_a, raw_a, jnp.float32, "add_raw")
    other = to_core(add_pieces(partial_b, comb_b, comb_b.dtype, "add_comb"))
    grad = over_chips(join_cores(partial_a, comb_a, other)).reshape(order, order)

    update = owner_update(refresh, grad, left, right, lroot, rroot)

    rows = over_chips(update.reshape(chips, 2, piece_rows, order))
    rows_a = pick_core(rows, 0, update)
    other = pick_core(rows, 1, rows_a)
    prev_a = to_next(rows_a)
    rows_b = to_core(other)
    next_b = to_prev(rows_b)
    prev_b, next_a = to_next(rows_b), to_prev(rows_a)
    over_a, over_b = to_next(prev_a), to_prev(next_b)
    new_left, new_right, new_lroot, new_rroot = owner_factors(
        rows_a, refresh, grad, left, right, lroot, rroot
    )
    over_a, over_b = to_next(prev_a), to_prev(next_b)
    updates = place_blocks(
        index,
        (rows_a, rows_b, prev_a, next_b, prev_b, next_a),
        ((0, 0), (0, 1), (3, 0), (1, 1), (3, 1), (1, 0)),
        "place_early",
    )
    updates = place_blocks(index, (over_a,), ((2, 0),), "place_over", updates)
    updates = place_blocks(index, (over_b,), ((2, 1),), "place_last", updates)
    return new_left[None], new_right[None], new_lroot[None], new_rroot[None], updates


def solution(mesh):
    owned = P(("dp", "fsdp"), None, None)
    return jax.shard_map(
        per_device,
        mesh=mesh,
        in_specs=(P("dp", None, "fsdp", None), owned, owned, owned, owned, P(), P()),
        out_specs=(owned, owned, owned, owned, P(None, "fsdp", None)),
        check_vma=False,
    )
```
